512 devices in a mesh: section: 8 (over z_lo), mp: 64 (over x, z_hi, y, core).
Axes of the slice: x: 4, y: 4, z: 16 (z_hi: 2, z_lo: 8; z = z_hi * 8 + z_lo), core: 2. Of those that a mesh axis runs over, the one named last changes fastest.
Arguments:
- latents: float32 [8, 64, 64, 96], P('section', 'mp'), may hold values from -6 to 6
- renoise: float32 [8, 64, 64, 96], P('section', 'mp'), may hold values from -6 to 6
- finished: float32 [64, 64, 96], P('mp', None, 'section'), may hold values from -6 to 6
- cache_keys: bfloat16 [64, 192, 768], P('mp'), may hold values from -160 to 160
- cache_values: bfloat16 [64, 192, 768], P('mp'), may hold values from -5 to 5
- window_start: int32 [64], P('mp'), may hold values from 0 to 5
- window_count: int32 [64], P('mp'), may hold values from 0 to 6, as said below
- timesteps: int32 [8], replicated, may hold values from 1 to 999, as said below
- w_in: bfloat16 [64, 1536], replicated, may hold values from -0.75 to 0.75
- w_time: bfloat16 [256, 7680], P(None, 'mp'), may hold values from -0.375 to 0.375
- w_qkv: bfloat16 [1536, 2304], P(('section', 'mp')), may hold values from -0.15625 to 0.15625
- wo_rows: bfloat16 [1536, 768], P('mp'), may hold values from -0.21875 to 0.21875
- w_out: bfloat16 [1536, 64], replicated, may hold values from -0.15625 to 0.15625
Outputs:
- next_latents: float32 [8, 64, 64, 96], P('section', 'mp')
The draws below stay inside these ranges and needn't reach their ends.
Inputs may be any that keep to these rules, and one draw needn't show every extreme that they name: `timesteps`: strictly decreasing along the steps; the first step's is 900 or more. `window_count`: some stream has all 6 frames valid and some stream none.
All inputs are finite; a program needn't handle non-finite values.
Results may differ from the reference program's by a relative error of at most 0.0065.
Values may be sent and summed in bfloat16 or wider, within the bound.
No kernel may reach another device: no remote copies, remote signals or barrier semaphores. Data moves between devices by JAX's collectives and lax.ppermute only.
A program may use at most 64 MiB of HBM per device.

```python
import math
import jax
import jax.numpy as jnp
from jax import lax

D = 1536
HEADS = 6
HEAD = 128
PATCH = 64
FREQ = 256
CACHE_FR = 6
FRAME_TOK = 32
INNER = 768
SPAN_TOK = 96
CACHE_TOK = 192
STEPS = 8
STREAMS = 64


def draw_cache_keys(key, part):
    key = jax.random.fold_in(key, 5)
    first_key = jax.random.fold_in(key, 0)
    shape_all = (STREAMS, CACHE_TOK, HEADS * HEAD)
    drawn = jnp.clip(jax.random.normal(first_key, shape_all, jnp.float32), -4.0, 4.0)
    return drawn.astype(jnp.bfloat16)


def draw_window_count(key, part):
    key = jax.random.fold_in(key, 7)
    first_key, second_key, third_key = jax.random.split(key, 3)
    frame_counts = jax.random.randint(first_key, (STREAMS,), 0, CACHE_FR + 1)
    full_stream = jax.random.randint(second_key, (), 0, STREAMS)
    empty_stream = (full_stream + 1 + jax.random.randint(third_key, (), 0, STREAMS - 1)) % STREAMS
    positions = jnp.arange(STREAMS)
    frame_counts = jnp.where(positions == full_stream, CACHE_FR, frame_counts)
    frame_counts = jnp.where(positions == empty_stream, 0, frame_counts)
    return frame_counts.astype(jnp.int32)


def draw_timesteps(key, part):
    key = jax.random.fold_in(key, 11)
    first_key, second_key = jax.random.split(key, 2)
    leading = jax.random.randint(first_key, (1,), 900, 1000)
    band_width = 1000 // STEPS
    jitter = jax.random.randint(second_key, (STEPS - 1,), 0, max(band_width // 2, 1))
    following = 1000 - band_width * jnp.arange(1, STEPS) - jitter
    return jnp.concatenate([leading, following]).astype(jnp.int32)


def with_ends(values, stream_key, least, largest):
    longest = values.shape.index(max(values.shape))
    spots = []
    for shift in (0, 1):
        where = [jax.random.randint(jax.random.fold_in(stream_key, axis), (), 0, length) for axis, length in enumerate(values.shape)]
        where[longest] = (where[longest] + shift) % values.shape[longest]
        spots.append(tuple(where))
    return values.at[spots[0]].set(least).at[spots[1]].set(largest)


def steps_of(stream_key, shape, cuts, least, high):
    level = 1.0
    for dim, shards_of in cuts:
        steps = jax.random.uniform(jax.random.fold_in(jax.random.fold_in(stream_key, 6), dim), (shards_of,), jnp.float32, least / len(cuts), high / len(cuts))
        level = level * jnp.repeat(jnp.exp(steps), shape[dim] // shards_of).reshape((-1,) + (1,) * (len(shape) - 1 - dim))
    return level


def bell_draw(key, dims, scale, bound, shards=(), held_as=jnp.bfloat16):
    values = jax.random.normal(key, dims, jnp.float32) * scale
    if len(shards) > 0:
        values = steps_of(key, dims, shards, -0.22, 0.18) * values
    return jnp.clip(values, min=-bound, max=bound).astype(held_as)


def setup_inputs(seed: int = 0) -> dict:
    splits = jax.random.split(jax.random.key(seed), 14)
    latents = bell_draw(splits[0], (STEPS, STREAMS, PATCH, SPAN_TOK), 1.0, 6.0, ((0, 8), (1, 64)), jnp.float32)
    renoise = bell_draw(splits[1], (STEPS, STREAMS, PATCH, SPAN_TOK), 1.0, 6.0, ((0, 8), (1, 64)), jnp.float32)
    finished = bell_draw(splits[2], (STREAMS, PATCH, SPAN_TOK), 1.0, 6.0, ((0, 64), (2, 8)), jnp.float32)
    cache_keys = draw_cache_keys(jax.random.fold_in(splits[13], 71), 0)
    cache_values = bell_draw(splits[4], (STREAMS, CACHE_TOK, INNER), 1.0, 5.0, ((0, 64),))
    window_start = with_ends(jax.random.randint(splits[5], (STREAMS,), 0, CACHE_FR), jax.random.fold_in(splits[5], 1), 0, CACHE_FR - 1).astype(jnp.int32)
    window_count = draw_window_count(jax.random.fold_in(splits[13], 71), 0)
    timesteps = draw_timesteps(jax.random.fold_in(splits[13], 71), 0)
    w_in = bell_draw(splits[8], (PATCH, D), PATCH ** -0.5, 0.75)
    w_time = bell_draw(splits[9], (FREQ, 5 * D), FREQ ** -0.5, 0.375, ((1, 64),))
    w_qkv = bell_draw(splits[10], (D, 3 * INNER), D ** -0.5, 0.15625, ((0, 512),))
    wo_rows = bell_draw(splits[11], (D, INNER), INNER ** -0.5, 0.21875, ((0, 64),))
    w_out = bell_draw(splits[12], (D, PATCH), D ** -0.5, 0.15625)
    return {"latents": latents, "renoise": renoise, "finished": finished, "cache_keys": cache_keys, "cache_values": cache_values, "window_start": window_start, "window_count": window_count, "timesteps": timesteps, "w_in": w_in, "w_time": w_time, "w_qkv": w_qkv, "wo_rows": wo_rows, "w_out": w_out}


def sinusoid(time_values, freq_count):
    half_count = freq_count // 2
    frequency = jnp.exp(-math.log(10000.0) * jnp.arange(half_count, dtype=jnp.float32) / half_count)
    phase_grid = time_values.astype(jnp.float32)[:, None] * frequency[None, :]
    return jnp.concatenate([jnp.cos(phase_grid), jnp.sin(phase_grid)], axis=1)

def layer_norm(values):
    middle = lax.optimization_barrier(jnp.mean(values, axis=-1, keepdims=True))
    centered = values - middle
    spread = lax.optimization_barrier(jnp.mean(centered * centered, axis=-1, keepdims=True))
    return centered * lax.rsqrt(spread + 1e-06)

def round_bf(values):
    return lax.optimization_barrier(values.astype(jnp.bfloat16)).astype(jnp.float32)

def attend(queries, key_rows, value_rows, key_mask, head_count):
    row_count, inner_width = queries.shape
    head_size = inner_width // head_count
    query_heads = queries.reshape(row_count, head_count, head_size)
    key_heads = key_rows.reshape(-1, head_count, head_size)
    value_heads = value_rows.reshape(-1, head_count, head_size)
    scores = jnp.einsum('qhe,khe->hqk', query_heads, key_heads) * (1.0 / math.sqrt(head_size))
    scores = jnp.where(key_mask[None, None, :], scores, -jnp.inf)
    highest = lax.optimization_barrier(jnp.max(scores, axis=-1, keepdims=True))
    weights = jnp.exp(scores - highest)
    probabilities = round_bf(weights / lax.optimization_barrier(jnp.sum(weights, axis=-1, keepdims=True)))
    mixture = jnp.einsum('hqk,khe->qhe', probabilities, value_heads)
    return round_bf(mixture.reshape(row_count, inner_width))

def reference(latents, renoise, finished, cache_keys, cache_values, window_start, window_count, timesteps, w_in, w_time, w_qkv, wo_rows, w_out):
    inner_width = HEADS * HEAD
    wide_time = w_time.astype(jnp.float32)
    patch_weights = w_in.astype(jnp.float32)
    qkv_weights = w_qkv.astype(jnp.float32)
    output_weights = wo_rows.astype(jnp.float32)
    head_weights = w_out.astype(jnp.float32)
    all_times = jnp.concatenate([timesteps, jnp.zeros((1,), jnp.int32)])
    modulations = jnp.dot(sinusoid(all_times, FREQ), wide_time, precision=lax.Precision.HIGHEST)
    rest_mod = modulations[STEPS]
    sigmas = all_times.astype(jnp.float32) / 1000.0
    frame_index = jnp.arange(CACHE_TOK) // FRAME_TOK
    own_mask = jnp.ones((2 * SPAN_TOK,), dtype=bool)

    def run_stream(pieces):
        stream_latents, stream_noise, stream_finished, stream_keys, stream_values, start_slot, count_slot = pieces
        keys_wide = stream_keys.astype(jnp.float32)
        values_wide = stream_values.astype(jnp.float32)
        fresh_hidden = jnp.einsum('pt,pd->td', round_bf(stream_finished), patch_weights)
        fresh_normed = round_bf(layer_norm(fresh_hidden) * (1.0 + rest_mod[D:2 * D]) + rest_mod[:D])
        finished_kv = round_bf(jnp.einsum('td,de->te', fresh_normed, qkv_weights[:, inner_width:]))
        valid_slots = (frame_index - start_slot + CACHE_FR) % CACHE_FR < count_slot
        key_mask = jnp.concatenate([valid_slots, own_mask], axis=0)
        stepped_all = []
        for step_index in range(STEPS):
            modulation = modulations[step_index]
            sigma_now = sigmas[step_index]
            sigma_next = sigmas[step_index + 1]
            current = stream_latents[step_index]
            noise = stream_noise[step_index]
            hidden = jnp.einsum('pt,pd->td', round_bf(current), patch_weights)
            normed = round_bf(layer_norm(hidden) * (1.0 + modulation[D:2 * D]) + modulation[:D])
            projected = round_bf(jnp.einsum('td,de->te', normed, qkv_weights))
            key_rows = jnp.concatenate([keys_wide, finished_kv[:, :inner_width], projected[:, inner_width:2 * inner_width]], axis=0)
            value_rows = jnp.concatenate([values_wide, finished_kv[:, inner_width:], projected[:, 2 * inner_width:]], axis=0)
            mixture = attend(projected[:, :inner_width], key_rows, value_rows, key_mask, HEADS)
            attended = jnp.einsum('ti,di->td', mixture, output_weights)
            hidden_after = hidden + modulation[2 * D:3 * D] * attended
            final_normed = round_bf(layer_norm(hidden_after) * (1.0 + modulation[4 * D:5 * D]) + modulation[3 * D:4 * D])
            velocity = jnp.einsum('td,dp->pt', final_normed, head_weights)
            stepped = (1.0 - sigma_next) * (current - sigma_now * velocity) + sigma_next * noise
            stepped_all.append(stepped)
        return jnp.stack([stepped_all[(target - 1) % STEPS] for target in range(STEPS)])
    outputs = lax.map(run_stream, (jnp.swapaxes(latents, 0, 1), jnp.swapaxes(renoise, 0, 1), finished, cache_keys, cache_values, window_start, window_count))
    return jnp.swapaxes(outputs, 0, 1)
```

```python
import math

import jax
import jax.numpy as jnp
from jax import lax
from jax.experimental import pallas as pl
from jax.experimental.pallas import tpu as pltpu
from jax.sharding import Mesh
from jax.sharding import PartitionSpec as P

HEADS = 6
HEAD = 128
CACHE_FR = 6
FRAME_TOK = 32
STEPS = 8
LANES = 128
QKV_BLOCKS = 18
KV_BLOCKS = 12
MSG_ROWS = 64
MOD_ROWS = 80
PLANE = ("x", "y", "c")
LINE = ("s", "w")
VMEM_LIMIT = 40 * 1024 * 1024

bf16 = jnp.bfloat16
f32 = jnp.float32


def product(left, right):
    return jnp.dot(left, right, preferred_element_type=f32)


def product_t(left, right):
    return lax.dot_general(left, right, (((1,), (1,)), ((), ())), preferred_element_type=f32)


def sinusoid(time_values, freq_count):
    half_count = freq_count // 2
    frequency = jnp.exp(-math.log(10000.0) * jnp.arange(half_count, dtype=f32) / half_count)
    phase_grid = time_values.astype(f32)[:, None] * frequency[None, :]
    return jnp.concatenate([jnp.cos(phase_grid), jnp.sin(phase_grid)], axis=1)


def pack_line(w_qkv_ref, finished_ref, embed_ref, w_time_ref, out_ref, held):
    rows = w_qkv_ref[...].astype(f32)
    for block in range(QKV_BLOCKS):
        held[3 * block : 3 * block + 3, :] = rows[:, block * LANES : (block + 1) * LANES]
    tokens = finished_ref[...].astype(bf16).astype(f32).T
    held[54:60, 0:64] = tokens[0:6]
    held[54:60, 64:128] = tokens[6:12]
    embed = embed_ref[...]
    w_time = w_time_ref[...]
    first = embed.astype(bf16)
    rest = embed - first.astype(f32)
    second = rest.astype(bf16)
    third = (rest - second.astype(f32)).astype(bf16)
    mods = product(first, w_time) + (product(second, w_time) + product(third, w_time))
    coarse = mods.astype(bf16).astype(f32)
    fine = mods - coarse
    held[60:64, :] = jnp.zeros((4, LANES), f32)
    held[62:63, 0:120] = coarse[STEPS : STEPS + 1]
    held[63:64, 0:120] = fine[STEPS : STEPS + 1]
    common = held[0:48, :].astype(bf16)
    for section in range(STEPS):
        step = (section - 1) % STEPS
        held[60:61, 0:120] = coarse[step : step + 1]
        held[61:62, 0:120] = fine[step : step + 1]
        last = held[48:64, :].astype(bf16)
        for side in range(2):
            out_ref[2 * section + side, 0:48, :] = common
            out_ref[2 * section + side, 48:64, :] = last


def pack_plane(side_ref, got_ref, out_ref, finished_ref, wide, tokens):
    side = side_ref[0]
    for peer in range(16):
        wide[peer * MSG_ROWS : (peer + 1) * MSG_ROWS, :] = got_ref[peer].astype(f32)
    for block in range(QKV_BLOCKS):
        for row in range(3):
            piece = wide[pl.ds(3 * block + row, 16, stride=MSG_ROWS), :].astype(bf16)
            out_ref[block, 16 * row : 16 * row + 16, :] = piece
            if block >= QKV_BLOCKS - KV_BLOCKS:
                out_ref[block + KV_BLOCKS, 16 * row : 16 * row + 16, :] = piece
            if block == QKV_BLOCKS - 1:
                out_ref[30, 16 * row : 16 * row + 16, :] = piece
                out_ref[31, 16 * row : 16 * row + 16, :] = piece
    mods = jnp.concatenate(
        [wide[60:64, :], wide[MSG_ROWS + 60 : MSG_ROWS + 64, :], jnp.zeros((8, LANES), f32)], axis=0
    ).astype(bf16)
    for target in range(32):
        out_ref[target, 48:64, :] = mods
    for section in range(STEPS):
        piece = wide[pl.ds(section * 2 * MSG_ROWS + side * MSG_ROWS + 54, 6), :]
        tokens[6 * section : 6 * section + 6, :] = piece[:, 0:64]
        tokens[48 + 6 * section : 54 + 6 * section, :] = piece[:, 64:128]
    finished_ref[...] = tokens[...].astype(bf16)


def flatten_mods(wide, kind, flat):
    groups = []
    for x in range(4):
        for w in range(2):
            begin = x * 8 * MSG_ROWS + 48 + w * 4 + 2 * kind
            groups.append(
                wide[pl.ds(begin, 8, stride=MSG_ROWS), :]
                + wide[pl.ds(begin + 1, 8, stride=MSG_ROWS), :]
            )
    runs = jnp.concatenate(groups, axis=0)
    place = lax.broadcasted_iota(jnp.int32, (64, LANES), 0) % 16
    lane = lax.broadcasted_iota(jnp.int32, (64, LANES), 1)
    for bit in range(4):
        turned = pltpu.roll(runs, LANES - 8 * 2**bit, axis=1)
        runs = jnp.where((place & 2**bit) != 0, turned, runs)
    runs = jnp.where(lane < 120 - 8 * place, runs, pltpu.roll(runs, 63, axis=0))
    for quarter in range(4):
        flat[15 * quarter : 15 * quarter + 15, :] = runs[16 * quarter : 16 * quarter + 15]
    flat[60:64, :] = jnp.zeros((4, LANES), f32)


def fold_block(block_ref, got_ref, w_in_ref, out_ref, mods_ref, wide, rows, scaled, flat_own, flat_rest):
    for peer in range(32):
        wide[peer * MSG_ROWS : (peer + 1) * MSG_ROWS, :] = got_ref[peer].astype(f32)
    for s in range(STEPS):
        for x in range(4):
            for w in range(2):
                for row in range(3):
                    rows[pl.ds(((s * 4 + x) * 2 + w) * 24 + row, 8, stride=3), :] = wide[
                        pl.ds(x * 8 * MSG_ROWS + row * 16 + s * 2 + w, 8, stride=MSG_ROWS), :
                    ]
    flatten_mods(wide, 0, flat_own)
    flatten_mods(wide, 1, flat_rest)
    mods_ref[...] = flat_own[...]
    at_rest = block_ref[0] >= QKV_BLOCKS
    used = jnp.where(at_rest, flat_rest[0:24, :], flat_own[0:24, :])
    turned = jnp.concatenate([used, jnp.zeros((LANES - 24, LANES), f32)], axis=0).T
    constant = jnp.zeros((8, LANES), f32)
    for part in range(12):
        piece = rows[part * LANES : (part + 1) * LANES, :]
        scaled[part * LANES : (part + 1) * LANES, :] = (
            piece * (1.0 + turned[:, 12 + part : 13 + part])
        ).astype(bf16)
        constant = constant + jnp.sum(
            (piece * turned[:, part : part + 1]).reshape(16, 8, LANES), axis=0
        )
    constant = jnp.sum(constant, axis=0, keepdims=True)
    w_in = w_in_ref[...]
    left = jnp.concatenate([w_in, jnp.ones((16, w_in.shape[1]), bf16)], axis=0)
    raw = product(left, scaled[...])
    middle = jnp.mean(w_in.astype(f32), axis=1, keepdims=True)
    linear = (raw[0:64] - middle * raw[64:65]).astype(bf16)
    coarse = constant.astype(bf16).astype(f32)
    tail = jnp.concatenate([coarse, constant - coarse, jnp.zeros((14, LANES), f32)], axis=0).astype(bf16)
    for target in range(32):
        out_ref[target, 0:64, :] = linear
        out_ref[target, 64:80, :] = tail


def spread_of(values):
    middle = jnp.mean(values, axis=-1, keepdims=True)
    centered = values - middle
    return centered, lax.rsqrt(jnp.mean(centered * centered, axis=-1, keepdims=True) + 1e-06)


def finish(
    window_ref,
    sigma_ref,
    got_ref,
    tokens_ref,
    state_ref,
    keys_ref,
    values_ref,
    mods_ref,
    w_in_ref,
    wo_ref,
    w_out_ref,
    out_ref,
    projected,
    mixture,
    after,
):
    current = state_ref[0:64, :]
    noise = state_ref[64:128, :]
    w_in = w_in_ref[...]
    tokens = current.T.astype(bf16)
    hidden = product(tokens, w_in)
    _, root = spread_of(hidden)
    done = tokens_ref[...]
    _, done_root = spread_of(product(done, w_in))

    def project(rows, factor, block):
        tail = got_ref[block, 64:80, :].astype(f32)
        return (product(rows, got_ref[block, 0:64, :]) * factor + (tail[0:1] + tail[1:2])).astype(bf16)

    start = window_ref[0]
    count = window_ref[1]
    frame = lax.broadcasted_iota(jnp.int32, (1, CACHE_FR * FRAME_TOK), 1) // FRAME_TOK
    frame = frame - start
    frame = jnp.where(frame < 0, frame + CACHE_FR, frame)
    bias = jnp.where(frame < count, 0.0, -jnp.inf)
    factor = 1.0 / math.sqrt(HEAD)
    for head in range(HEADS):
        columns = slice(head * HEAD, (head + 1) * HEAD)
        query = project(tokens, root, head)
        own_key = project(tokens, root, HEADS + head)
        own_value = project(tokens, root, 2 * HEADS + head)
        done_key = project(done, done_root, 3 * HEADS + head)
        done_value = project(done, done_root, 4 * HEADS + head)
        held = product_t(query, keys_ref[:, columns]) * factor + bias
        own = product_t(query, own_key) * factor
        last = product_t(query, done_key) * factor
        highest = jnp.maximum(
            jnp.max(held, axis=-1, keepdims=True),
            jnp.maximum(jnp.max(own, axis=-1, keepdims=True), jnp.max(last, axis=-1, keepdims=True)),
        )
        held = jnp.exp(held - highest)
        own = jnp.exp(own - highest)
        last = jnp.exp(last - highest)
        total = (
            jnp.sum(held, axis=-1, keepdims=True)
            + jnp.sum(own, axis=-1, keepdims=True)
            + jnp.sum(last, axis=-1, keepdims=True)
        )
        share = 1.0 / total
        mixture[:, columns] = (
            product((held * share).astype(bf16), values_ref[:, columns])
            + product((own * share).astype(bf16), own_value)
            + product((last * share).astype(bf16), done_value)
        ).astype(bf16)
    mixed = mixture[...]
    sums = jnp.zeros((tokens.shape[0], LANES), f32)
    for part in range(12):
        columns = slice(part * LANES, (part + 1) * LANES)
        attended = product_t(mixed, wo_ref[columns, :])
        value = hidden[:, columns] + mods_ref[24 + part : 25 + part, :] * attended
        after[:, columns] = value
        sums = sums + value
    width = 12 * LANES
    middle = jnp.sum(sums, axis=-1, keepdims=True) * (1.0 / width)
    sums = jnp.zeros((tokens.shape[0], LANES), f32)
    for part in range(12):
        columns = slice(part * LANES, (part + 1) * LANES)
        value = after[:, columns] - middle
        sums = sums + value * value
    root = lax.rsqrt(jnp.sum(sums, axis=-1, keepdims=True) * (1.0 / width) + 1e-06)
    for part in range(12):
        columns = slice(part * LANES, (part + 1) * LANES)
        value = (after[:, columns] - middle) * root
        projected[:, columns] = (
            value * (1.0 + mods_ref[48 + part : 49 + part, :]) + mods_ref[36 + part : 37 + part, :]
        ).astype(bf16)
    velocity = product(projected[...], w_out_ref[...]).T
    sigma_now = sigma_ref[0]
    sigma_next = sigma_ref[1]
    out_ref[...] = (1.0 - sigma_next) * (current - sigma_now * velocity) + sigma_next * noise


def whole(count):
    return [pl.BlockSpec(memory_space=pltpu.VMEM)] * count


def scalars(count):
    return [pl.BlockSpec(memory_space=pltpu.SMEM)] * count


def per_device(
    latents,
    renoise,
    finished,
    cache_keys,
    cache_values,
    window_start,
    window_count,
    timesteps,
    w_in,
    w_time,
    w_qkv,
    wo_rows,
    w_out,
):
    section = lax.axis_index("s")
    step = (section + STEPS - 1) % STEPS
    params = pltpu.CompilerParams(vmem_limit_bytes=VMEM_LIMIT)

    state = jnp.concatenate([latents[0, 0], renoise[0, 0]], axis=0)
    state = lax.ppermute(state, "s", [(i, (i + 1) % STEPS) for i in range(STEPS)])
    wo_all = lax.all_gather(wo_rows, ("x", "w", "y", "c"), axis=0, tiled=True)

    times = jnp.concatenate([timesteps, jnp.zeros((STEPS,), jnp.int32)])
    embed = sinusoid(times, w_time.shape[0])
    message = pl.pallas_call(
        pack_line,
        out_shape=jax.ShapeDtypeStruct((16, MSG_ROWS, LANES), bf16),
        in_specs=whole(4),
        out_specs=pl.BlockSpec(memory_space=pltpu.VMEM),
        scratch_shapes=[pltpu.VMEM((MSG_ROWS, LANES), f32)],
        compiler_params=params,
        name="pack_line",
    )(w_qkv, finished[0], embed, w_time)
    got = lax.all_to_all(message, LINE, 0, 0, tiled=True)

    side = lax.axis_index("w").astype(jnp.int32)[None]
    message, tokens = pl.pallas_call(
        pack_plane,
        out_shape=[
            jax.ShapeDtypeStruct((32, MSG_ROWS, LANES), bf16),
            jax.ShapeDtypeStruct((96, 64), bf16),
        ],
        in_specs=scalars(1) + whole(1),
        out_specs=whole(2),
        scratch_shapes=[pltpu.VMEM((16 * MSG_ROWS, LANES), f32), pltpu.VMEM((96, 64), f32)],
        compiler_params=params,
        name="pack_plane",
    )(side, got)
    got = lax.all_to_all(message, PLANE, 0, 0, tiled=True)

    block = lax.axis_index(PLANE).astype(jnp.int32)[None]
    message, mods = pl.pallas_call(
        fold_block,
        out_shape=[
            jax.ShapeDtypeStruct((32, MOD_ROWS, LANES), bf16),
            jax.ShapeDtypeStruct((64, LANES), f32),
        ],
        in_specs=scalars(1) + whole(2),
        out_specs=whole(2),
        scratch_shapes=[
            pltpu.VMEM((32 * MSG_ROWS, LANES), f32),
            pltpu.VMEM((1536, LANES), f32),
            pltpu.VMEM((1536, LANES), bf16),
            pltpu.VMEM((64, LANES), f32),
            pltpu.VMEM((64, LANES), f32),
        ],
        compiler_params=params,
        name="fold_block",
    )(block, got, w_in)
    got = lax.all_to_all(message, PLANE, 0, 0, tiled=True)

    time_now = timesteps[step]
    time_next = jnp.where(step + 1 < STEPS, timesteps[jnp.minimum(step + 1, STEPS - 1)], 0)
    sigma = jnp.stack([time_now, time_next]).astype(f32) / 1000.0
    window = jnp.concatenate([window_start, window_count])
    stepped = pl.pallas_call(
        finish,
        out_shape=jax.ShapeDtypeStruct((64, 96), f32),
        in_specs=scalars(2) + whole(9),
        out_specs=pl.BlockSpec(memory_space=pltpu.VMEM),
        scratch_shapes=[
            pltpu.VMEM((96, 1536), bf16),
            pltpu.VMEM((96, 768), bf16),
            pltpu.VMEM((96, 1536), f32),
        ],
        compiler_params=params,
        name="finish",
    )(window, sigma, got, tokens, state, cache_keys[0], cache_values[0], mods, w_in, wo_all, w_out)
    return stepped[None, None]


def solution(mesh):
    grid = Mesh(mesh.devices.reshape(8, 4, 2, 4, 2), ("s", "x", "w", "y", "c"))
    streams = ("x", "w", "y", "c")
    in_specs = (
        P("s", streams, None, None),
        P("s", streams, None, None),
        P(streams, None, "s"),
        P(streams, None, None),
        P(streams, None, None),
        P(streams),
        P(streams),
        P(),
        P(),
        P(None, streams),
        P(("s",) + streams, None),
        P(streams, None),
        P(),
    )
    out_specs = P("s", streams, None, None)
    return jax.shard_map(
        per_device, mesh=grid, in_specs=in_specs, out_specs=out_specs, check_vma=False
    )
```

```python
import math

import jax
import jax.numpy as jnp
from jax import lax
from jax.experimental import pallas as pl
from jax.experimental.pallas import tpu as pltpu
from jax.sharding import Mesh
from jax.sharding import PartitionSpec as P

HEADS = 6
HEAD = 128
CACHE_FR = 6
FRAME_TOK = 32
STEPS = 8
LANES = 128
QKV_BLOCKS = 18
KV_BLOCKS = 12
LINE_ROWS = 88
MSG_ROWS = 64
PLANE_ROWS = 208
MOD_ROWS = 80
PLANE = ("x", "y", "c")
LINE = ("s", "w")
VMEM_LIMIT = 16 * 1024 * 1024

bf16 = jnp.bfloat16
f32 = jnp.float32


def product(left, right):
    return jnp.dot(left, right, preferred_element_type=f32)


def product_t(left, right):
    return lax.dot_general(left, right, (((1,), (1,)), ((), ())), preferred_element_type=f32)


def pack_line(times_ref, *refs):
    out_ref, held, wo_held, w_qkv_ref, finished_ref, w_time_ref, wo_ref, arrived = refs[4:]
    copies = [
        pltpu.make_async_copy(source, target, arrived.at[place])
        for place, (source, target) in enumerate(zip(refs[:4], refs[7:11]))
    ]
    for copy in copies:
        copy.start()
    place = lax.broadcasted_iota(jnp.int32, (16, LANES), 0)
    times = jnp.zeros((16, LANES), f32)
    for step in range(STEPS):
        times = jnp.where(place == step, times_ref[step].astype(f32), times)
    lane = lax.broadcasted_iota(jnp.int32, (16, LANES), 1).astype(f32)
    phase = times * jnp.exp(-math.log(10000.0) * lane / LANES)
    embed = jnp.concatenate([jnp.cos(phase), jnp.sin(phase)], axis=1)
    for copy in copies:
        copy.wait()
    rows = w_qkv_ref[...].astype(f32)
    for block in range(QKV_BLOCKS):
        held[3 * block : 3 * block + 3, :] = rows[:, block * LANES : (block + 1) * LANES]
    tokens = finished_ref[...].reshape(12, 64).astype(bf16).astype(f32)
    held[54:60, 0:64] = tokens[0:6]
    held[54:60, 64:128] = tokens[6:12]
    w_time = w_time_ref[...]
    first = embed.astype(bf16)
    rest = embed - first.astype(f32)
    second = rest.astype(bf16)
    third = (rest - second.astype(f32)).astype(bf16)
    mods = product_t(first, w_time) + (product_t(second, w_time) + product_t(third, w_time))
    coarse = mods.astype(bf16).astype(f32)
    fine = mods - coarse
    held[60:64, :] = jnp.zeros((4, LANES), f32)
    held[62:63, 0:120] = coarse[STEPS : STEPS + 1]
    held[63:64, 0:120] = fine[STEPS : STEPS + 1]
    wo = wo_ref[...].astype(f32)
    section = lax.axis_index("s")
    for block in range(HEADS):
        wo_held[24 * block : 24 * block + 24, :] = wo[:, block * LANES : (block + 1) * LANES]
        held[64 + 3 * block : 67 + 3 * block, :] = wo_held[pl.ds(24 * block + 3 * section, 3), :]
    held[82:88, :] = jnp.zeros((6, LANES), f32)
    common = held[0:48, :].astype(bf16)
    wo_rows = held[64:88, :].astype(bf16)
    for section in range(STEPS):
        step = (section - 1) % STEPS
        held[60:61, 0:120] = coarse[step : step + 1]
        held[61:62, 0:120] = fine[step : step + 1]
        last = held[48:64, :].astype(bf16)
        for side in range(2):
            out_ref[2 * section + side, 0:48, :] = common
            out_ref[2 * section + side, 48:64, :] = last
            out_ref[2 * section + side, 64:88, :] = wo_rows


def pack_plane(got_ref, out_ref, finished_ref, wide, tokens, wo):
    side = lax.axis_index("w")
    for peer in range(16):
        wide[peer * LINE_ROWS : (peer + 1) * LINE_ROWS, :] = got_ref[peer].astype(f32)
    for block in range(QKV_BLOCKS):
        for row in range(3):
            piece = wide[pl.ds(3 * block + row, 16, stride=LINE_ROWS), :].astype(bf16)
            out_ref[block, 16 * row : 16 * row + 16, :] = piece
            if block >= QKV_BLOCKS - KV_BLOCKS:
                out_ref[block + KV_BLOCKS, 16 * row : 16 * row + 16, :] = piece
            if block == QKV_BLOCKS - 1:
                out_ref[30, 16 * row : 16 * row + 16, :] = piece
                out_ref[31, 16 * row : 16 * row + 16, :] = piece
    mods = jnp.concatenate(
        [wide[60:64, :], wide[LINE_ROWS + 60 : LINE_ROWS + 64, :], jnp.zeros((8, LANES), f32)], axis=0
    ).astype(bf16)
    for half in range(2):
        for block in range(HEADS):
            for row in range(3):
                wo[pl.ds(144 * half + 24 * block + row, 8, stride=3), :] = wide[
                    pl.ds(half * LINE_ROWS + 64 + 3 * block + row, 8, stride=2 * LINE_ROWS), :
                ]
    halves = [wo[144 * half : 144 * (half + 1), :].astype(bf16) for half in range(2)]
    for target in range(32):
        out_ref[target, 48:64, :] = mods
        out_ref[target, 64:208, :] = halves[target % 2]
    for section in range(STEPS):
        piece = wide[pl.ds(section * 2 * LINE_ROWS + side * LINE_ROWS + 54, 6), :]
        tokens[6 * section : 6 * section + 6, :] = piece[:, 0:64]
        tokens[48 + 6 * section : 54 + 6 * section, :] = piece[:, 64:128]
    finished_ref[...] = tokens[...].astype(bf16)


def flatten_mods(wide, kind, flat):
    groups = []
    for x in range(4):
        for w in range(2):
            begin = x * 8 * MSG_ROWS + 48 + w * 4 + 2 * kind
            groups.append(
                wide[pl.ds(begin, 8, stride=MSG_ROWS), :]
                + wide[pl.ds(begin + 1, 8, stride=MSG_ROWS), :]
            )
    runs = jnp.concatenate(groups, axis=0)
    place = lax.broadcasted_iota(jnp.int32, (64, LANES), 0) % 16
    lane = lax.broadcasted_iota(jnp.int32, (64, LANES), 1)
    for bit in range(4):
        turned = pltpu.roll(runs, LANES - 8 * 2**bit, axis=1)
        runs = jnp.where((place & 2**bit) != 0, turned, runs)
    runs = jnp.where(lane < 120 - 8 * place, runs, pltpu.roll(runs, 63, axis=0))
    for quarter in range(4):
        flat[15 * quarter : 15 * quarter + 15, :] = runs[16 * quarter : 16 * quarter + 15]
    flat[60:64, :] = jnp.zeros((4, LANES), f32)


def fold_block(got_ref, w_in_ref, state_ref, out_ref, mods_ref, wide, rows, scaled, flat_own, flat_rest):
    for peer in range(32):
        wide[peer * MSG_ROWS : (peer + 1) * MSG_ROWS, :] = got_ref[peer, 0:MSG_ROWS, :].astype(f32)
    for s in range(STEPS):
        for x in range(4):
            for w in range(2):
                for row in range(3):
                    rows[pl.ds(((s * 4 + x) * 2 + w) * 24 + row, 8, stride=3), :] = wide[
                        pl.ds(x * 8 * MSG_ROWS + row * 16 + s * 2 + w, 8, stride=MSG_ROWS), :
                    ]
    flatten_mods(wide, 0, flat_own)
    flatten_mods(wide, 1, flat_rest)
    mods_ref[...] = flat_own[...]
    at_rest = lax.axis_index(PLANE) >= QKV_BLOCKS
    used = jnp.where(at_rest, flat_rest[0:24, :], flat_own[0:24, :])
    turned = jnp.concatenate([used, jnp.zeros((LANES - 24, LANES), f32)], axis=0).T
    constant = jnp.zeros((8, LANES), f32)
    for part in range(12):
        piece = rows[part * LANES : (part + 1) * LANES, :]
        scaled[part * LANES : (part + 1) * LANES, :] = (
            piece * (1.0 + turned[:, 12 + part : 13 + part])
        ).astype(bf16)
        constant = constant + jnp.sum(
            (piece * turned[:, part : part + 1]).reshape(16, 8, LANES), axis=0
        )
    constant = jnp.sum(constant, axis=0, keepdims=True)
    w_in = w_in_ref[...]
    left = jnp.concatenate([w_in, jnp.ones((16, w_in.shape[1]), bf16)], axis=0)
    raw = product(left, scaled[...])
    middle = jnp.mean(w_in.astype(f32), axis=1, keepdims=True)
    linear = (raw[0:64] - middle * raw[64:65]).astype(bf16)
    coarse = constant.astype(bf16).astype(f32)
    tail = jnp.concatenate([coarse, constant - coarse, jnp.zeros((14, LANES), f32)], axis=0).astype(bf16)
    for target in range(32):
        out_ref[target, 0:64, :] = linear
        out_ref[target, 64:80, :] = tail


def spread_of(values):
    middle = jnp.mean(values, axis=-1, keepdims=True)
    centered = values - middle
    return centered, lax.rsqrt(jnp.mean(centered * centered, axis=-1, keepdims=True) + 1e-06)


def unpack_wo(got_ref, mods_ref, out_ref):
    for pair in range(16):
        first = got_ref[2 * pair, 64:208, :].astype(f32)
        second = got_ref[2 * pair + 1, 64:208, :].astype(f32)
        for block in range(HEADS):
            rows = slice(24 * block, 24 * block + 24)
            out_ref[48 * pair : 48 * pair + 48, block * LANES : (block + 1) * LANES] = jnp.concatenate(
                [first[rows], second[rows]], axis=0
            ).astype(bf16)


def sigmas(times_ref):
    step = lax.rem(lax.axis_index("s") + STEPS - 1, STEPS)
    now = times_ref[step].astype(f32) * 0.001
    after = times_ref[lax.rem(step + 1, STEPS)].astype(f32) * 0.001
    return now, jnp.where(step == STEPS - 1, 0.0, after)


def finish(
    start_ref,
    count_ref,
    times_ref,
    got_ref,
    held_refs,
    wo_refs,
    out_ref,
    normed,
    mixture,
    after,
    state_ref,
    w_in_ref,
    tokens_ref,
    keys_ref,
    values_ref,
    mods_ref,
    w_out_ref,
    wo,
    arrived,
):
    near = (state_ref, w_in_ref, tokens_ref, keys_ref, values_ref, mods_ref, w_out_ref)
    copies = [
        pltpu.make_async_copy(source, target, arrived.at[place])
        for place, (source, target) in enumerate(zip(held_refs, near))
    ]
    core = lax.axis_index("c")
    for half, side in enumerate((core, 1 - core)):
        for x in range(4):
            begin = pl.multiple_of(384 * x + 192 * side, 192)
            source, place = (wo_refs[0], x) if half == 0 else (wo_refs[1 + x // 2], x % 2)
            copies.append(
                pltpu.make_async_copy(
                    source.at[192 * place : 192 * (place + 1)],
                    wo.at[pl.ds(begin, 192)],
                    arrived.at[len(copies)],
                )
            )
    for copy in copies:
        copy.start()
    for copy in copies[:3]:
        copy.wait()
    current = state_ref[0:64, :]
    w_in = w_in_ref[...]
    tokens = current.T.astype(bf16)
    hidden = product(tokens, w_in)
    _, root = spread_of(hidden)
    done = tokens_ref[...]
    _, done_root = spread_of(product(done, w_in))

    def project(rows, factor, block):
        tail = got_ref[block, 64:80, :].astype(f32)
        return (product(rows, got_ref[block, 0:64, :]) * factor + (tail[0:1] + tail[1:2])).astype(bf16)

    start = start_ref[0]
    count = count_ref[0]
    frame = lax.broadcasted_iota(jnp.int32, (1, CACHE_FR * FRAME_TOK), 1) // FRAME_TOK
    frame = frame - start
    frame = jnp.where(frame < 0, frame + CACHE_FR, frame)
    bias = jnp.where(frame < count, 0.0, -jnp.inf)
    factor = 1.0 / math.sqrt(HEAD)
    for copy in copies[3:5]:
        copy.wait()
    for head in range(HEADS):
        columns = slice(head * HEAD, (head + 1) * HEAD)
        query = project(tokens, root, head)
        own_key = project(tokens, root, HEADS + head)
        own_value = project(tokens, root, 2 * HEADS + head)
        done_key = project(done, done_root, 3 * HEADS + head)
        done_value = project(done, done_root, 4 * HEADS + head)
        held = product_t(query, keys_ref[:, columns]) * factor + bias
        own = product_t(query, own_key) * factor
        last = product_t(query, done_key) * factor
        highest = jnp.maximum(
            jnp.max(held, axis=-1, keepdims=True),
            jnp.maximum(jnp.max(own, axis=-1, keepdims=True), jnp.max(last, axis=-1, keepdims=True)),
        )
        held = jnp.exp(held - highest)
        own = jnp.exp(own - highest)
        last = jnp.exp(last - highest)
        total = (
            jnp.sum(held, axis=-1, keepdims=True)
            + jnp.sum(own, axis=-1, keepdims=True)
            + jnp.sum(last, axis=-1, keepdims=True)
        )
        share = 1.0 / total
        mixture[:, columns] = (
            product((held * share).astype(bf16), values_ref[:, columns])
            + product((own * share).astype(bf16), own_value)
            + product((last * share).astype(bf16), done_value)
        ).astype(bf16)
    mixed = mixture[...]
    for copy in copies[5:]:
        copy.wait()
    sums = jnp.zeros((tokens.shape[0], LANES), f32)
    for part in range(12):
        columns = slice(part * LANES, (part + 1) * LANES)
        attended = product_t(mixed, wo[columns, :])
        value = hidden[:, columns] + mods_ref[24 + part : 25 + part, :] * attended
        after[:, columns] = value
        sums = sums + value
    width = 12 * LANES
    middle = jnp.sum(sums, axis=-1, keepdims=True) * (1.0 / width)
    sums = jnp.zeros((tokens.shape[0], LANES), f32)
    for part in range(12):
        columns = slice(part * LANES, (part + 1) * LANES)
        value = after[:, columns] - middle
        sums = sums + value * value
    root = lax.rsqrt(jnp.sum(sums, axis=-1, keepdims=True) * (1.0 / width) + 1e-06)
    for part in range(12):
        columns = slice(part * LANES, (part + 1) * LANES)
        value = (after[:, columns] - middle) * root
        normed[:, columns] = (value * (1.0 + mods_ref[48 + part : 49 + part, :]) + mods_ref[36 + part : 37 + part, :]).astype(bf16)
    velocity = product_t(w_out_ref[...], normed[...])
    sigma_now, sigma_next = sigmas(times_ref)
    out_ref[...] = (1.0 - sigma_next) * (current - sigma_now * velocity) + sigma_next * state_ref[64:128, :]


def whole(count):
    return [pl.BlockSpec(memory_space=pltpu.VMEM)] * count


def scalars(count):
    return [pl.BlockSpec(memory_space=pltpu.SMEM)] * count


def anywhere(count):
    return [pl.BlockSpec(memory_space=pltpu.HBM)] * count


def in_hbm(array):
    return pltpu.with_memory_space_constraint(array, pltpu.HBM)


def in_vmem(array):
    return pltpu.with_memory_space_constraint(array, pltpu.VMEM)


def shifted(array, axis, by):
    size = lax.axis_size(axis)
    return lax.ppermute(array, axis, [(i, (i - by) % size) for i in range(size)])


def per_device(
    latents,
    renoise,
    finished,
    cache_keys,
    cache_values,
    window_start,
    window_count,
    timesteps,
    w_in,
    w_time,
    w_qkv,
    wo_rows,
    w_out,
):
    params = pltpu.CompilerParams(vmem_limit_bytes=VMEM_LIMIT)

    message = pl.pallas_call(
        pack_line,
        out_shape=pltpu.VMEM((16, LINE_ROWS, LANES), bf16),
        in_specs=scalars(1) + anywhere(4),
        out_specs=pl.BlockSpec(memory_space=pltpu.VMEM),
        scratch_shapes=[
            pltpu.VMEM((LINE_ROWS, LANES), f32),
            pltpu.VMEM((144, LANES), f32),
            pltpu.VMEM(w_qkv.shape, bf16),
            pltpu.VMEM((12, 1, 64), f32),
            pltpu.VMEM((120, 256), bf16),
            pltpu.VMEM(wo_rows.shape, bf16),
            pltpu.SemaphoreType.DMA((4,)),
        ],
        compiler_params=params,
        name="pack_line",
    )(timesteps, *map(in_hbm, (w_qkv, jnp.transpose(finished, (2, 0, 1)), w_time.T, wo_rows)))
    got = lax.all_to_all(message, LINE, 0, 0, tiled=True)

    state = shifted(jnp.concatenate([latents[0, 0], renoise[0, 0]], axis=0), "s", -1)
    message, tokens = pl.pallas_call(
        pack_plane,
        out_shape=[
            pltpu.VMEM((32, PLANE_ROWS, LANES), bf16),
            pltpu.HBM((96, 64), bf16),
        ],
        in_specs=whole(1),
        out_specs=whole(2),
        scratch_shapes=[
            pltpu.VMEM((16 * LINE_ROWS, LANES), f32),
            pltpu.VMEM((96, 64), f32),
            pltpu.VMEM((288, LANES), f32),
        ],
        compiler_params=params,
        name="pack_plane",
    )(in_vmem(got))
    got = lax.all_to_all(message, PLANE, 0, 0, tiled=True)

    message, mods = pl.pallas_call(
        fold_block,
        out_shape=[
            pltpu.VMEM((32, MOD_ROWS, LANES), bf16),
            pltpu.HBM((64, LANES), f32),
        ],
        in_specs=whole(2) + anywhere(1),
        out_specs=whole(2),
        scratch_shapes=[
            pltpu.VMEM((32 * MSG_ROWS, LANES), f32),
            pltpu.VMEM((1536, LANES), f32),
            pltpu.VMEM((1536, LANES), bf16),
            pltpu.VMEM((64, LANES), f32),
            pltpu.VMEM((64, LANES), f32),
        ],
        compiler_params=params,
        name="fold_block",
    )(in_vmem(got), w_in, in_hbm(state))
    wo_half = pl.pallas_call(
        unpack_wo,
        out_shape=pltpu.VMEM((768, 768), bf16),
        in_specs=whole(1) + anywhere(1),
        out_specs=pl.BlockSpec(memory_space=pltpu.VMEM),
        compiler_params=params,
        name="unpack_wo",
    )(in_vmem(got), in_hbm(mods))
    wo_other = [shifted(wo_half[384 * part : 384 * (part + 1)], "c", 1) for part in range(2)]
    got = lax.all_to_all(message, PLANE, 0, 0, tiled=True)

    stepped = pl.pallas_call(
        lambda *refs: finish(*refs[:4], refs[4:11], refs[11:14], *refs[14:]),
        out_shape=jax.ShapeDtypeStruct((64, 96), f32),
        in_specs=scalars(3) + whole(1) + anywhere(10),
        out_specs=pl.BlockSpec(memory_space=pltpu.VMEM),
        scratch_shapes=[
            pltpu.VMEM((96, 1536), bf16),
            pltpu.VMEM((96, 768), bf16),
            pltpu.VMEM((96, 1536), f32),
            pltpu.VMEM((128, 96), f32),
            pltpu.VMEM((64, 1536), bf16),
            pltpu.VMEM((96, 64), bf16),
            pltpu.VMEM((192, 768), bf16),
            pltpu.VMEM((192, 768), bf16),
            pltpu.VMEM((64, LANES), f32),
            pltpu.VMEM((64, 1536), bf16),
            pltpu.VMEM((1536, 768), bf16),
            pltpu.SemaphoreType.DMA((15,)),
        ],
        compiler_params=params,
        name="finish",
    )(
        window_start,
        window_count,
        timesteps,
        in_vmem(got),
        *map(
            in_hbm,
            (state, w_in, tokens, cache_keys[0], cache_values[0], mods, w_out.T, wo_half, *wo_other),
        ),
    )
    return stepped[None, None]


def solution(mesh):
    grid = Mesh(mesh.devices.reshape(8, 4, 2, 4, 2), ("s", "x", "w", "y", "c"))
    streams = ("x", "w", "y", "c")
    in_specs = (
        P("s", streams, None, None),
        P("s", streams, None, None),
        P(streams, None, "s"),
        P(streams, None, None),
        P(streams, None, None),
        P(streams),
        P(streams),
        P(),
        P(),
        P(None, streams),
        P(("s",) + streams, None),
        P(streams, None),
        P(),
    )
    out_specs = P("s", streams, None, None)
    return jax.shard_map(
        per_device, mesh=grid, in_specs=in_specs, out_specs=out_specs, check_vma=False
    )
```

```python
import math

import jax
import jax.numpy as jnp
from jax import lax
from jax.experimental import pallas as pl
from jax.experimental.pallas import tpu as pltpu
from jax.sharding import Mesh
from jax.sharding import PartitionSpec as P

HEADS = 6
HEAD = 128
CACHE_FR = 6
FRAME_TOK = 32
STEPS = 8
LANES = 128
QKV_BLOCKS = 18
KV_BLOCKS = 12
LINE_ROWS = 88
MSG_ROWS = 56
PLANE_ROWS = 200
MOD_ROWS = 80
PLANE = ("x", "y", "c")
LINE = ("s", "w")
VMEM_LIMIT = 16 * 1024 * 1024

bf16 = jnp.bfloat16
f32 = jnp.float32


def product(left, right):
    return jnp.dot(left, right, preferred_element_type=f32)


def product_t(left, right):
    return lax.dot_general(left, right, (((1,), (1,)), ((), ())), preferred_element_type=f32)


def pack_line(*refs):
    out_ref, held, wo_held, times_ref, w_qkv_ref, finished_ref, w_time_ref, wo_ref, arrived = refs[5:]
    copies = [
        pltpu.make_async_copy(source, target, arrived.at[place])
        for place, (source, target) in enumerate(zip(refs[:5], refs[8:13]))
    ]
    for copy in copies:
        copy.start()
    copies[0].wait()
    place = lax.broadcasted_iota(jnp.int32, (16, LANES), 0)
    times = jnp.zeros((16, LANES), f32)
    for step in range(STEPS):
        times = jnp.where(place == step, times_ref[step].astype(f32), times)
    lane = lax.broadcasted_iota(jnp.int32, (16, LANES), 1).astype(f32)
    phase = times * jnp.exp(-math.log(10000.0) * lane / LANES)
    embed = jnp.concatenate([jnp.cos(phase), jnp.sin(phase)], axis=1)
    for copy in copies[1:]:
        copy.wait()
    rows = w_qkv_ref[...].astype(f32)
    for block in range(QKV_BLOCKS):
        held[3 * block : 3 * block + 3, :] = rows[:, block * LANES : (block + 1) * LANES]
    tokens = finished_ref[...].reshape(12, 64).astype(bf16).astype(f32)
    held[54:60, 0:64] = tokens[0:6]
    held[54:60, 64:128] = tokens[6:12]
    w_time = w_time_ref[...]
    first = embed.astype(bf16)
    rest = embed - first.astype(f32)
    second = rest.astype(bf16)
    third = (rest - second.astype(f32)).astype(bf16)
    mods = product_t(first, w_time) + (product_t(second, w_time) + product_t(third, w_time))
    coarse = mods.astype(bf16).astype(f32)
    fine = mods - coarse
    held[60:64, :] = jnp.zeros((4, LANES), f32)
    held[62:63, 0:120] = coarse[STEPS : STEPS + 1]
    held[63:64, 0:120] = fine[STEPS : STEPS + 1]
    wo = wo_ref[...].astype(f32)
    section = lax.axis_index("s")
    for block in range(HEADS):
        wo_held[24 * block : 24 * block + 24, :] = wo[:, block * LANES : (block + 1) * LANES]
        held[64 + 3 * block : 67 + 3 * block, :] = wo_held[pl.ds(24 * block + 3 * section, 3), :]
    held[82:88, :] = jnp.zeros((6, LANES), f32)
    common = held[0:48, :].astype(bf16)
    wo_rows = held[64:88, :].astype(bf16)
    for section in range(STEPS):
        step = (section - 1) % STEPS
        held[60:61, 0:120] = coarse[step : step + 1]
        held[61:62, 0:120] = fine[step : step + 1]
        last = held[48:64, :].astype(bf16)
        for side in range(2):
            out_ref[2 * section + side, 0:48, :] = common
            out_ref[2 * section + side, 48:64, :] = last
            out_ref[2 * section + side, 64:88, :] = wo_rows


def pack_plane(got_ref, out_ref, finished_ref, wide, tokens, wo):
    side = lax.axis_index("w")
    for peer in range(16):
        wide[peer * LINE_ROWS : (peer + 1) * LINE_ROWS, :] = got_ref[peer].astype(f32)
    for block in range(QKV_BLOCKS):
        for row in range(3):
            piece = wide[pl.ds(3 * block + row, 16, stride=LINE_ROWS), :].astype(bf16)
            out_ref[block, 16 * row : 16 * row + 16, :] = piece
            if block >= QKV_BLOCKS - KV_BLOCKS:
                out_ref[block + KV_BLOCKS, 16 * row : 16 * row + 16, :] = piece
            if block == QKV_BLOCKS - 1:
                out_ref[30, 16 * row : 16 * row + 16, :] = piece
                out_ref[31, 16 * row : 16 * row + 16, :] = piece
    mods = jnp.concatenate(
        [wide[60:64, :], wide[LINE_ROWS + 60 : LINE_ROWS + 64, :]], axis=0
    ).astype(bf16)
    for half in range(2):
        for block in range(HEADS):
            for row in range(3):
                wo[pl.ds(144 * half + 24 * block + row, 8, stride=3), :] = wide[
                    pl.ds(half * LINE_ROWS + 64 + 3 * block + row, 8, stride=2 * LINE_ROWS), :
                ]
    halves = [wo[144 * half : 144 * (half + 1), :].astype(bf16) for half in range(2)]
    for target in range(32):
        out_ref[target, 48:56, :] = mods
        out_ref[target, 56:200, :] = halves[target % 2]
    for section in range(STEPS):
        piece = wide[pl.ds(section * 2 * LINE_ROWS + side * LINE_ROWS + 54, 6), :]
        tokens[6 * section : 6 * section + 6, :] = piece[:, 0:64]
        tokens[48 + 6 * section : 54 + 6 * section, :] = piece[:, 64:128]
    finished_ref[...] = tokens[...].astype(bf16)


def flatten_mods(wide, kind, flat):
    groups = []
    for x in range(4):
        for w in range(2):
            begin = x * 8 * MSG_ROWS + 48 + w * 4 + 2 * kind
            groups.append(
                wide[pl.ds(begin, 8, stride=MSG_ROWS), :]
                + wide[pl.ds(begin + 1, 8, stride=MSG_ROWS), :]
            )
    runs = jnp.concatenate(groups, axis=0)
    place = lax.broadcasted_iota(jnp.int32, (64, LANES), 0) % 16
    lane = lax.broadcasted_iota(jnp.int32, (64, LANES), 1)
    for bit in range(4):
        turned = pltpu.roll(runs, LANES - 8 * 2**bit, axis=1)
        runs = jnp.where((place & 2**bit) != 0, turned, runs)
    runs = jnp.where(lane < 120 - 8 * place, runs, pltpu.roll(runs, 63, axis=0))
    for quarter in range(4):
        flat[15 * quarter : 15 * quarter + 15, :] = runs[16 * quarter : 16 * quarter + 15]
    flat[60:64, :] = jnp.zeros((4, LANES), f32)


def fold_block(got_ref, w_in_ref, state_ref, out_ref, mods_ref, wide, rows, scaled, flat_own, flat_rest):
    for peer in range(32):
        wide[peer * MSG_ROWS : (peer + 1) * MSG_ROWS, :] = got_ref[peer, 0:MSG_ROWS, :].astype(f32)
    for s in range(STEPS):
        for x in range(4):
            for w in range(2):
                for row in range(3):
                    rows[pl.ds(((s * 4 + x) * 2 + w) * 24 + row, 8, stride=3), :] = wide[
                        pl.ds(x * 8 * MSG_ROWS + row * 16 + s * 2 + w, 8, stride=MSG_ROWS), :
                    ]
    flatten_mods(wide, 0, flat_own)
    flatten_mods(wide, 1, flat_rest)
    mods_ref[...] = flat_own[...]
    at_rest = lax.axis_index(PLANE) >= QKV_BLOCKS
    used = jnp.where(at_rest, flat_rest[0:24, :], flat_own[0:24, :])
    turned = jnp.concatenate([used, jnp.zeros((LANES - 24, LANES), f32)], axis=0).T
    constant = jnp.zeros((8, LANES), f32)
    for part in range(12):
        piece = rows[part * LANES : (part + 1) * LANES, :]
        scaled[part * LANES : (part + 1) * LANES, :] = (
            piece * (1.0 + turned[:, 12 + part : 13 + part])
        ).astype(bf16)
        constant = constant + jnp.sum(
            (piece * turned[:, part : part + 1]).reshape(16, 8, LANES), axis=0
        )
    constant = jnp.sum(constant, axis=0, keepdims=True)
    w_in = w_in_ref[...]
    left = jnp.concatenate([w_in, jnp.ones((16, w_in.shape[1]), bf16)], axis=0)
    raw = product(left, scaled[...])
    middle = jnp.mean(w_in.astype(f32), axis=1, keepdims=True)
    linear = (raw[0:64] - middle * raw[64:65]).astype(bf16)
    coarse = constant.astype(bf16).astype(f32)
    tail = jnp.concatenate([coarse, constant - coarse, jnp.zeros((14, LANES), f32)], axis=0).astype(bf16)
    for target in range(32):
        out_ref[target, 0:64, :] = linear
        out_ref[target, 64:80, :] = tail


def spread_of(values):
    middle = jnp.mean(values, axis=-1, keepdims=True)
    centered = values - middle
    return centered, lax.rsqrt(jnp.mean(centered * centered, axis=-1, keepdims=True) + 1e-06)


def unpack_wo(got_ref, mods_ref, out_ref):
    for pair in range(16):
        first = got_ref[2 * pair, 56:200, :].astype(f32)
        second = got_ref[2 * pair + 1, 56:200, :].astype(f32)
        for block in range(HEADS):
            rows = slice(24 * block, 24 * block + 24)
            out_ref[48 * pair : 48 * pair + 48, block * LANES : (block + 1) * LANES] = jnp.concatenate(
                [first[rows], second[rows]], axis=0
            ).astype(bf16)


def sigmas(times_ref):
    step = lax.rem(lax.axis_index("s") + STEPS - 1, STEPS)
    now = times_ref[step].astype(f32) * 0.001
    after = times_ref[lax.rem(step + 1, STEPS)].astype(f32) * 0.001
    return now, jnp.where(step == STEPS - 1, 0.0, after)


def finish(
    start_ref,
    count_ref,
    got_ref,
    held_refs,
    wo_refs,
    out_ref,
    queries,
    keys,
    values,
    mixture,
    after,
    normed,
    state_ref,
    w_in_ref,
    tokens_ref,
    mods_ref,
    w_out_ref,
    times_ref,
    wo,
    arrived,
):
    cached = CACHE_FR * FRAME_TOK
    near = (state_ref, w_in_ref, tokens_ref, keys.at[0:cached], values.at[0:cached])
    near = near + (mods_ref, w_out_ref, times_ref)
    copies = [
        pltpu.make_async_copy(source, target, arrived.at[place])
        for place, (source, target) in enumerate(zip(held_refs, near))
    ]
    core = lax.axis_index("c")
    for half, side in enumerate((core, 1 - core)):
        for x in range(4):
            begin = pl.multiple_of(384 * x + 192 * side, 192)
            source, place = (wo_refs[0], x) if half == 0 else (wo_refs[1 + x // 2], x % 2)
            copies.append(
                pltpu.make_async_copy(
                    source.at[192 * place : 192 * (place + 1)],
                    wo.at[pl.ds(begin, 192)],
                    arrived.at[len(copies)],
                )
            )
    for copy in copies:
        copy.start()
    for copy in copies[:3]:
        copy.wait()
    current = state_ref[0:64, :]
    w_in = w_in_ref[...]
    tokens = current.T.astype(bf16)
    hidden = product(tokens, w_in)
    _, root = spread_of(hidden)
    done = tokens_ref[...]
    _, done_root = spread_of(product(done, w_in))

    def project(rows, factor, first):
        linear = jnp.concatenate([got_ref[first + head, 0:64, :] for head in range(HEADS)], axis=1)
        tail = jnp.concatenate([got_ref[first + head, 64:72, :] for head in range(HEADS)], axis=1).astype(f32)
        return (product(rows, linear) * factor + (tail[0:1] + tail[1:2])).astype(bf16)

    queries[...] = project(tokens, root, 0)
    keys[cached + 96 :, :] = project(tokens, root, HEADS)
    values[cached + 96 :, :] = project(tokens, root, 2 * HEADS)
    keys[cached : cached + 96, :] = project(done, done_root, 3 * HEADS)
    values[cached : cached + 96, :] = project(done, done_root, 4 * HEADS)
    for copy in copies[3:5]:
        copy.wait()
    frame = lax.broadcasted_iota(jnp.int32, (1, cached + 192), 1) // FRAME_TOK
    turned = frame - start_ref[0]
    turned = jnp.where(turned < 0, turned + CACHE_FR, turned)
    bias = jnp.where((frame >= CACHE_FR) | (turned < count_ref[0]), 0.0, -jnp.inf)
    factor = 1.0 / (math.sqrt(HEAD) * math.log(2.0))
    for head in range(HEADS):
        columns = slice(head * HEAD, (head + 1) * HEAD)
        scores = product_t(queries[:, columns], keys[:, columns]) + bias
        scores = jnp.exp2((scores - jnp.max(scores, axis=-1, keepdims=True)) * factor)
        share = 1.0 / jnp.sum(scores, axis=-1, keepdims=True)
        mixture[:, columns] = (product(scores.astype(bf16), values[:, columns]) * share).astype(bf16)
    mixed = mixture[...]
    for copy in copies[5:]:
        copy.wait()
    sums = jnp.zeros((tokens.shape[0], LANES), f32)
    for part in range(12):
        columns = slice(part * LANES, (part + 1) * LANES)
        attended = product_t(mixed, wo[columns, :])
        value = hidden[:, columns] + mods_ref[24 + part : 25 + part, :] * attended
        after[:, columns] = value
        sums = sums + value
    width = 12 * LANES
    middle = jnp.sum(sums, axis=-1, keepdims=True) * (1.0 / width)
    sums = jnp.zeros((tokens.shape[0], LANES), f32)
    for part in range(12):
        columns = slice(part * LANES, (part + 1) * LANES)
        value = after[:, columns] - middle
        sums = sums + value * value
    root = lax.rsqrt(jnp.sum(sums, axis=-1, keepdims=True) * (1.0 / width) + 1e-06)
    for part in range(12):
        columns = slice(part * LANES, (part + 1) * LANES)
        value = (after[:, columns] - middle) * root
        normed[:, columns] = (
            value * (1.0 + mods_ref[48 + part : 49 + part, :]) + mods_ref[36 + part : 37 + part, :]
        ).astype(bf16)
    velocity = product_t(w_out_ref[...], normed[...])
    sigma_now, sigma_next = sigmas(times_ref)
    out_ref[...] = (1.0 - sigma_next) * (current - sigma_now * velocity) + sigma_next * state_ref[64:128, :]


def whole(count):
    return [pl.BlockSpec(memory_space=pltpu.VMEM)] * count


def scalars(count):
    return [pl.BlockSpec(memory_space=pltpu.SMEM)] * count


def anywhere(count):
    return [pl.BlockSpec(memory_space=pltpu.HBM)] * count


def in_hbm(array):
    return pltpu.with_memory_space_constraint(array, pltpu.HBM)


def in_vmem(array):
    return pltpu.with_memory_space_constraint(array, pltpu.VMEM)


def shifted(array, axis, by):
    size = lax.axis_size(axis)
    return lax.ppermute(array, axis, [(i, (i - by) % size) for i in range(size)])


def per_device(
    latents,
    renoise,
    finished,
    cache_keys,
    cache_values,
    window_start,
    window_count,
    timesteps,
    w_in,
    w_time,
    w_qkv,
    wo_rows,
    w_out,
):
    params = pltpu.CompilerParams(vmem_limit_bytes=VMEM_LIMIT)

    message = pl.pallas_call(
        pack_line,
        out_shape=pltpu.VMEM((16, LINE_ROWS, LANES), bf16),
        in_specs=anywhere(5),
        out_specs=pl.BlockSpec(memory_space=pltpu.VMEM),
        scratch_shapes=[
            pltpu.VMEM((LINE_ROWS, LANES), f32),
            pltpu.VMEM((144, LANES), f32),
            pltpu.SMEM((STEPS,), jnp.int32),
            pltpu.VMEM(w_qkv.shape, bf16),
            pltpu.VMEM((12, 1, 64), f32),
            pltpu.VMEM((120, 256), bf16),
            pltpu.VMEM(wo_rows.shape, bf16),
            pltpu.SemaphoreType.DMA((5,)),
        ],
        compiler_params=params,
        name="pack_line",
    )(*map(in_hbm, (timesteps, w_qkv, jnp.transpose(finished, (2, 0, 1)), w_time.T, wo_rows)))
    got = lax.all_to_all(message, LINE, 0, 0, tiled=True)

    state = shifted(jnp.concatenate([latents[0, 0], renoise[0, 0]], axis=0), "s", -1)
    message, tokens = pl.pallas_call(
        pack_plane,
        out_shape=[
            pltpu.VMEM((32, PLANE_ROWS, LANES), bf16),
            pltpu.HBM((96, 64), bf16),
        ],
        in_specs=whole(1),
        out_specs=whole(2),
        scratch_shapes=[
            pltpu.VMEM((16 * LINE_ROWS, LANES), f32),
            pltpu.VMEM((96, 64), f32),
            pltpu.VMEM((288, LANES), f32),
        ],
        compiler_params=params,
        name="pack_plane",
    )(in_vmem(got))
    got = lax.all_to_all(message, PLANE, 0, 0, tiled=True)

    message, mods = pl.pallas_call(
        fold_block,
        out_shape=[
            pltpu.VMEM((32, MOD_ROWS, LANES), bf16),
            pltpu.HBM((64, LANES), f32),
        ],
        in_specs=whole(2) + anywhere(1),
        out_specs=whole(2),
        scratch_shapes=[
            pltpu.VMEM((32 * MSG_ROWS, LANES), f32),
            pltpu.VMEM((1536, LANES), f32),
            pltpu.VMEM((1536, LANES), bf16),
            pltpu.VMEM((64, LANES), f32),
            pltpu.VMEM((64, LANES), f32),
        ],
        compiler_params=params,
        name="fold_block",
    )(in_vmem(got), w_in, in_hbm(state))
    wo_half = pl.pallas_call(
        unpack_wo,
        out_shape=pltpu.VMEM((768, 768), bf16),
        in_specs=whole(1) + anywhere(1),
        out_specs=pl.BlockSpec(memory_space=pltpu.VMEM),
        compiler_params=params,
        name="unpack_wo",
    )(in_vmem(got), in_hbm(mods))
    wo_other = [shifted(wo_half[384 * part : 384 * (part + 1)], "c", 1) for part in range(2)]
    got = lax.all_to_all(message, PLANE, 0, 0, tiled=True)

    stepped = pl.pallas_call(
        lambda *refs: finish(*refs[:3], refs[3:11], refs[11:14], *refs[14:]),
        out_shape=jax.ShapeDtypeStruct((64, 96), f32),
        in_specs=scalars(2) + whole(1) + anywhere(8) + [pl.BlockSpec(memory_space=pl.ANY)] * 3,
        out_specs=pl.BlockSpec(memory_space=pltpu.VMEM),
        scratch_shapes=[
            pltpu.VMEM((96, 768), bf16),
            pltpu.VMEM((384, 768), bf16),
            pltpu.VMEM((384, 768), bf16),
            pltpu.VMEM((96, 768), bf16),
            pltpu.VMEM((96, 1536), f32),
            pltpu.VMEM((96, 1536), bf16),
            pltpu.VMEM((128, 96), f32),
            pltpu.VMEM((64, 1536), bf16),
            pltpu.VMEM((96, 64), bf16),
            pltpu.VMEM((64, LANES), f32),
            pltpu.VMEM((64, 1536), bf16),
            pltpu.SMEM((STEPS,), jnp.int32),
            pltpu.VMEM((1536, 768), bf16),
            pltpu.SemaphoreType.DMA((16,)),
        ],
        compiler_params=params,
        name="finish",
    )(
        window_start,
        window_count,
        in_vmem(got),
        *map(
            in_hbm,
            (
                state,
                w_in,
                tokens,
                cache_keys[0],
                cache_values[0],
                mods,
                w_out.T,
                timesteps,
            ),
        ),
        wo_half,
        *wo_other,
    )
    return stepped[None, None]


def solution(mesh):
    grid = Mesh(mesh.devices.reshape(8, 4, 2, 4, 2), ("s", "x", "w", "y", "c"))
    streams = ("x", "w", "y", "c")
    in_specs = (
        P("s", streams, None, None),
        P("s", streams, None, None),
        P(streams, None, "s"),
        P(streams, None, None),
        P(streams, None, None),
        P(streams),
        P(streams),
        P(),
        P(),
        P(None, streams),
        P(("s",) + streams, None),
        P(streams, None),
        P(),
    )
    out_specs = P("s", streams, None, None)
    return jax.shard_map(
        per_device, mesh=grid, in_specs=in_specs, out_specs=out_specs, check_vma=False
    )
```

```python
import math

import jax
import jax.numpy as jnp
from jax import lax
from jax.experimental import pallas as pl
from jax.experimental.pallas import tpu as pltpu
from jax.sharding import Mesh
from jax.sharding import PartitionSpec as P

HEADS = 6
HEAD = 128
CACHE_FR = 6
FRAME_TOK = 32
STEPS = 8
LANES = 128
QKV_BLOCKS = 18
KV_BLOCKS = 12
LINE_ROWS = 72
MSG_ROWS = 56
PLANE_ROWS = 128
MOD_ROWS = 80
PLANE = ("x", "y", "c")
LINE = ("s", "w")
VMEM_LIMIT = 16 * 1024 * 1024

bf16 = jnp.bfloat16
f32 = jnp.float32


def product(left, right):
    return jnp.dot(left, right, preferred_element_type=f32)


def product_t(left, right):
    return lax.dot_general(left, right, (((1,), (1,)), ((), ())), preferred_element_type=f32)


def pack_line(*refs):
    out_ref, held, wo_held, times_ref, w_qkv_ref, finished_ref, w_time_ref, wo_ref, arrived = refs[5:]
    copies = [
        pltpu.make_async_copy(source, target, arrived.at[place])
        for place, (source, target) in enumerate(zip(refs[:5], refs[8:13]))
    ]
    for copy in copies:
        copy.start()
    copies[0].wait()
    place = lax.broadcasted_iota(jnp.int32, (16, LANES), 0)
    times = jnp.zeros((16, LANES), f32)
    for step in range(STEPS):
        times = jnp.where(place == step, times_ref[step].astype(f32), times)
    lane = lax.broadcasted_iota(jnp.int32, (16, LANES), 1).astype(f32)
    phase = times * jnp.exp(-math.log(10000.0) * lane / LANES)
    embed = jnp.concatenate([jnp.cos(phase), jnp.sin(phase)], axis=1)
    for copy in copies[1:]:
        copy.wait()
    rows = w_qkv_ref[...].astype(f32)
    for block in range(QKV_BLOCKS):
        held[3 * block : 3 * block + 3, :] = rows[:, block * LANES : (block + 1) * LANES]
    tokens = finished_ref[...].reshape(12, 64).astype(bf16).astype(f32)
    tokens = jnp.concatenate([tokens[0:6], tokens[6:12]], axis=1)
    tokens = jnp.concatenate([tokens, jnp.zeros((3, LANES), f32)], axis=0)
    w_time = w_time_ref[...]
    first = embed.astype(bf16)
    rest = embed - first.astype(f32)
    second = rest.astype(bf16)
    third = (rest - second.astype(f32)).astype(bf16)
    mods = product_t(first, w_time) + (product_t(second, w_time) + product_t(third, w_time))
    coarse = mods.astype(bf16).astype(f32)
    fine = mods - coarse
    held[54:72, :] = jnp.zeros((18, LANES), f32)
    held[56:57, 0:120] = coarse[STEPS : STEPS + 1]
    held[57:58, 0:120] = fine[STEPS : STEPS + 1]
    wo = wo_ref[...].astype(f32)
    own_section, own_side = lax.axis_index("s"), lax.axis_index("w")
    share = []
    for block in range(HEADS):
        wo_held[24 * block : 24 * block + 24, :] = wo[:, block * LANES : (block + 1) * LANES]
        share.append(wo_held[pl.ds(24 * block + 3 * own_section, 3), :])
    share = [jnp.concatenate(share[0:3], axis=0), jnp.concatenate(share[3:6], axis=0)]
    common = held[0:48, :].astype(bf16)
    for section in range(STEPS):
        step = (section - 1) % STEPS
        held[54:55, 0:120] = coarse[step : step + 1]
        held[55:56, 0:120] = fine[step : step + 1]
        for side in range(2):
            held[58:67, :] = jnp.where(own_side == side, tokens, share[section % 2])
            out_ref[2 * section + side, 0:48, :] = common
            out_ref[2 * section + side, 48:72, :] = held[48:72, :].astype(bf16)


def pack_plane(got_ref, wo_ref, out_ref, finished_ref, wide, tokens, far, near, arrived):
    columns = pl.ds(pl.multiple_of(384 * lax.rem(lax.axis_index("s"), 2), LANES), 384)
    copy = pltpu.make_async_copy(wo_ref.at[:, columns], near, arrived)
    copy.start()
    side = lax.axis_index("w")
    for peer in range(16):
        wide[peer * LINE_ROWS : (peer + 1) * LINE_ROWS, :] = got_ref[peer].astype(f32)
    for block in range(QKV_BLOCKS):
        for row in range(3):
            piece = wide[pl.ds(3 * block + row, 16, stride=LINE_ROWS), :].astype(bf16)
            out_ref[block, 16 * row : 16 * row + 16, :] = piece
            if block >= QKV_BLOCKS - KV_BLOCKS:
                out_ref[block + KV_BLOCKS, 16 * row : 16 * row + 16, :] = piece
            if block == QKV_BLOCKS - 1:
                out_ref[30, 16 * row : 16 * row + 16, :] = piece
                out_ref[31, 16 * row : 16 * row + 16, :] = piece
    mods = jnp.concatenate(
        [wide[54:58, :], wide[LINE_ROWS + 54 : LINE_ROWS + 58, :]], axis=0
    ).astype(bf16)
    for block in range(3):
        for row in range(3):
            begin = (1 - side) * LINE_ROWS + 58 + 3 * block + row
            far[pl.ds(24 * block + row, 8, stride=3), :] = wide[pl.ds(begin, 8, stride=2 * LINE_ROWS), :]
    copy.wait()
    here = near[...].astype(f32)
    here = jnp.concatenate([here[:, block * LANES : (block + 1) * LANES] for block in range(3)], axis=0)
    there = far[...]
    halves = [jnp.where(side == half, here, there).astype(bf16) for half in range(2)]
    for target in range(32):
        out_ref[target, 48:56, :] = mods
        out_ref[target, 56:128, :] = halves[target % 2]
    for section in range(STEPS):
        piece = wide[pl.ds(section * 2 * LINE_ROWS + side * LINE_ROWS + 58, 6), :]
        tokens[6 * section : 6 * section + 6, :] = piece[:, 0:64]
        tokens[48 + 6 * section : 54 + 6 * section, :] = piece[:, 64:128]
    finished_ref[...] = tokens[...].astype(bf16)


def flatten_mods(wide, kind, flat):
    groups = []
    for x in range(4):
        for w in range(2):
            begin = x * 8 * MSG_ROWS + 48 + w * 4 + 2 * kind
            groups.append(
                wide[pl.ds(begin, 8, stride=MSG_ROWS), :]
                + wide[pl.ds(begin + 1, 8, stride=MSG_ROWS), :]
            )
    runs = jnp.concatenate(groups, axis=0)
    place = lax.broadcasted_iota(jnp.int32, (64, LANES), 0) % 16
    lane = lax.broadcasted_iota(jnp.int32, (64, LANES), 1)
    for bit in range(4):
        turned = pltpu.roll(runs, LANES - 8 * 2**bit, axis=1)
        runs = jnp.where((place & 2**bit) != 0, turned, runs)
    runs = jnp.where(lane < 120 - 8 * place, runs, pltpu.roll(runs, 63, axis=0))
    for quarter in range(4):
        flat[15 * quarter : 15 * quarter + 15, :] = runs[16 * quarter : 16 * quarter + 15]
    flat[60:64, :] = jnp.zeros((4, LANES), f32)


def fold_block(got_ref, w_in_ref, state_ref, out_ref, mods_ref, wide, rows, scaled, flat_own, flat_rest):
    for peer in range(32):
        wide[peer * MSG_ROWS : (peer + 1) * MSG_ROWS, :] = got_ref[peer, 0:MSG_ROWS, :].astype(f32)
    for s in range(STEPS):
        for x in range(4):
            for w in range(2):
                for row in range(3):
                    rows[pl.ds(((s * 4 + x) * 2 + w) * 24 + row, 8, stride=3), :] = wide[
                        pl.ds(x * 8 * MSG_ROWS + row * 16 + s * 2 + w, 8, stride=MSG_ROWS), :
                    ]
    flatten_mods(wide, 0, flat_own)
    flatten_mods(wide, 1, flat_rest)
    mods_ref[...] = flat_own[...]
    at_rest = lax.axis_index(PLANE) >= QKV_BLOCKS
    used = jnp.where(at_rest, flat_rest[0:24, :], flat_own[0:24, :])
    turned = jnp.concatenate([used, jnp.zeros((LANES - 24, LANES), f32)], axis=0).T
    constant = jnp.zeros((8, LANES), f32)
    for part in range(12):
        piece = rows[part * LANES : (part + 1) * LANES, :]
        scaled[part * LANES : (part + 1) * LANES, :] = (
            piece * (1.0 + turned[:, 12 + part : 13 + part])
        ).astype(bf16)
        constant = constant + jnp.sum(
            (piece * turned[:, part : part + 1]).reshape(16, 8, LANES), axis=0
        )
    constant = jnp.sum(constant, axis=0, keepdims=True)
    w_in = w_in_ref[...]
    left = jnp.concatenate([w_in, jnp.ones((16, w_in.shape[1]), bf16)], axis=0)
    raw = product(left, scaled[...])
    middle = jnp.mean(w_in.astype(f32), axis=1, keepdims=True)
    linear = (raw[0:64] - middle * raw[64:65]).astype(bf16)
    coarse = constant.astype(bf16).astype(f32)
    tail = jnp.concatenate([coarse, constant - coarse, jnp.zeros((14, LANES), f32)], axis=0).astype(bf16)
    for target in range(32):
        out_ref[target, 0:64, :] = linear
        out_ref[target, 64:80, :] = tail


def spread_of(values):
    middle = jnp.mean(values, axis=-1, keepdims=True)
    centered = values - middle
    return centered, lax.rsqrt(jnp.mean(centered * centered, axis=-1, keepdims=True) + 1e-06)


def unpack_wo(got_ref, mods_ref, out_ref):
    for pair in range(16):
        first = got_ref[2 * pair, 56:128, :].astype(f32)
        second = got_ref[2 * pair + 1, 56:128, :].astype(f32)
        for block in range(3):
            rows = slice(24 * block, 24 * block + 24)
            out_ref[48 * pair : 48 * pair + 48, block * LANES : (block + 1) * LANES] = jnp.concatenate(
                [first[rows], second[rows]], axis=0
            ).astype(bf16)


def sigmas(times_ref):
    step = lax.rem(lax.axis_index("s") + STEPS - 1, STEPS)
    now = times_ref[step].astype(f32) * 0.001
    after = times_ref[lax.rem(step + 1, STEPS)].astype(f32) * 0.001
    return now, jnp.where(step == STEPS - 1, 0.0, after)


def finish(
    start_ref,
    count_ref,
    got_ref,
    state_ref,
    w_in_ref,
    held_refs,
    wo_refs,
    out_ref,
    queries,
    keys,
    values,
    mixture,
    after,
    normed,
    tokens_ref,
    mods_ref,
    w_out_ref,
    times_ref,
    wo,
    arrived,
):
    cached = CACHE_FR * FRAME_TOK
    near = (tokens_ref, keys.at[0:cached], values.at[0:cached], mods_ref, w_out_ref, times_ref)
    copies = [
        pltpu.make_async_copy(source, target, arrived.at[place])
        for place, (source, target) in enumerate(zip(held_refs, near))
    ]
    core, odd = lax.axis_index("c"), lax.rem(lax.axis_index("s"), 2)
    for source, side, half in zip(wo_refs, (core, core, 1 - core, 1 - core), (odd, 1 - odd) * 2):
        columns = pl.ds(pl.multiple_of(384 * half, LANES), 384)
        for x in range(4):
            rows = pl.ds(pl.multiple_of(384 * x + 192 * side, 192), 192)
            copies.append(
                pltpu.make_async_copy(
                    source.at[192 * x : 192 * (x + 1)], wo.at[rows, columns], arrived.at[len(copies)]
                )
            )
    for copy in copies:
        copy.start()
    current = state_ref[0:64, :]
    w_in = w_in_ref[...]
    tokens = current.T.astype(bf16)
    hidden = product(tokens, w_in)
    _, root = spread_of(hidden)
    copies[0].wait()
    done = tokens_ref[...]
    _, done_root = spread_of(product(done, w_in))

    def project(rows, factor, first):
        linear = jnp.concatenate([got_ref[first + head, 0:64, :] for head in range(HEADS)], axis=1)
        tail = jnp.concatenate([got_ref[first + head, 64:72, :] for head in range(HEADS)], axis=1).astype(f32)
        return (product(rows, linear) * factor + (tail[0:1] + tail[1:2])).astype(bf16)

    queries[...] = project(tokens, root, 0)
    keys[cached + 96 :, :] = project(tokens, root, HEADS)
    values[cached + 96 :, :] = project(tokens, root, 2 * HEADS)
    keys[cached : cached + 96, :] = project(done, done_root, 3 * HEADS)
    values[cached : cached + 96, :] = project(done, done_root, 4 * HEADS)
    for copy in copies[1:3]:
        copy.wait()
    frame = lax.broadcasted_iota(jnp.int32, (1, cached + 192), 1) // FRAME_TOK
    turned = frame - start_ref[0]
    turned = jnp.where(turned < 0, turned + CACHE_FR, turned)
    bias = jnp.where((frame >= CACHE_FR) | (turned < count_ref[0]), 0.0, -jnp.inf)
    factor = 1.0 / (math.sqrt(HEAD) * math.log(2.0))
    for head in range(HEADS):
        columns = slice(head * HEAD, (head + 1) * HEAD)
        scores = product_t(queries[:, columns], keys[:, columns]) + bias
        scores = jnp.exp2((scores - jnp.max(scores, axis=-1, keepdims=True)) * factor)
        share = 1.0 / jnp.sum(scores, axis=-1, keepdims=True)
        mixture[:, columns] = (product(scores.astype(bf16), values[:, columns]) * share).astype(bf16)
    mixed = mixture[...]
    for copy in copies[3:]:
        copy.wait()
    sums = jnp.zeros((tokens.shape[0], LANES), f32)
    for part in range(12):
        columns = slice(part * LANES, (part + 1) * LANES)
        attended = product_t(mixed, wo[columns, :])
        value = hidden[:, columns] + mods_ref[24 + part : 25 + part, :] * attended
        after[:, columns] = value
        sums = sums + value
    width = 12 * LANES
    middle = jnp.sum(sums, axis=-1, keepdims=True) * (1.0 / width)
    sums = jnp.zeros((tokens.shape[0], LANES), f32)
    for part in range(12):
        columns = slice(part * LANES, (part + 1) * LANES)
        value = after[:, columns] - middle
        sums = sums + value * value
    root = lax.rsqrt(jnp.sum(sums, axis=-1, keepdims=True) * (1.0 / width) + 1e-06)
    for part in range(12):
        columns = slice(part * LANES, (part + 1) * LANES)
        value = (after[:, columns] - middle) * root
        normed[:, columns] = (
            value * (1.0 + mods_ref[48 + part : 49 + part, :]) + mods_ref[36 + part : 37 + part, :]
        ).astype(bf16)
    velocity = product_t(w_out_ref[...], normed[...])
    sigma_now, sigma_next = sigmas(times_ref)
    out_ref[...] = (1.0 - sigma_next) * (current - sigma_now * velocity) + sigma_next * state_ref[64:128, :]


def whole(count):
    return [pl.BlockSpec(memory_space=pltpu.VMEM)] * count


def scalars(count):
    return [pl.BlockSpec(memory_space=pltpu.SMEM)] * count


def anywhere(count):
    return [pl.BlockSpec(memory_space=pltpu.HBM)] * count


def in_hbm(array):
    return pltpu.with_memory_space_constraint(array, pltpu.HBM)


def in_vmem(array):
    return pltpu.with_memory_space_constraint(array, pltpu.VMEM)


def shifted(array, axis, by):
    size = lax.axis_size(axis)
    return lax.ppermute(array, axis, [(i, (i - by) % size) for i in range(size)])


def neighbour_planes():
    def place(chip, core):
        return (chip % 8 * 2 + chip // 8) * 2 + core

    return [
        (place(chip, core), place((chip + 1 if (chip + core) % 2 == 0 else chip - 1) % 16, core))
        for chip in range(16)
        for core in range(2)
    ]


def per_device(
    latents,
    renoise,
    finished,
    cache_keys,
    cache_values,
    window_start,
    window_count,
    timesteps,
    w_in,
    w_time,
    w_qkv,
    wo_rows,
    w_out,
):
    params = pltpu.CompilerParams(vmem_limit_bytes=VMEM_LIMIT)

    message = pl.pallas_call(
        pack_line,
        out_shape=pltpu.VMEM((16, LINE_ROWS, LANES), bf16),
        in_specs=anywhere(5),
        out_specs=pl.BlockSpec(memory_space=pltpu.VMEM),
        scratch_shapes=[
            pltpu.VMEM((LINE_ROWS, LANES), f32),
            pltpu.VMEM((144, LANES), f32),
            pltpu.SMEM((STEPS,), jnp.int32),
            pltpu.VMEM(w_qkv.shape, bf16),
            pltpu.VMEM((12, 1, 64), f32),
            pltpu.VMEM((120, 256), bf16),
            pltpu.VMEM(wo_rows.shape, bf16),
            pltpu.SemaphoreType.DMA((5,)),
        ],
        compiler_params=params,
        name="pack_line",
    )(*map(in_hbm, (timesteps, w_qkv, jnp.transpose(finished, (2, 0, 1)), w_time.T, wo_rows)))
    got = lax.all_to_all(message, LINE, 0, 0, tiled=True)

    state = shifted(jnp.concatenate([latents[0, 0], renoise[0, 0]], axis=0), "s", -1)
    message, tokens = pl.pallas_call(
        pack_plane,
        out_shape=[
            pltpu.VMEM((32, PLANE_ROWS, LANES), bf16),
            pltpu.HBM((96, 64), bf16),
        ],
        in_specs=whole(1) + anywhere(1),
        out_specs=whole(2),
        scratch_shapes=[
            pltpu.VMEM((16 * LINE_ROWS, LANES), f32),
            pltpu.VMEM((96, 64), f32),
            pltpu.VMEM((72, LANES), f32),
            pltpu.VMEM((24, 384), bf16),
            pltpu.SemaphoreType.DMA(()),
        ],
        compiler_params=params,
        name="pack_plane",
    )(in_vmem(got), in_hbm(wo_rows))
    got = lax.all_to_all(message, PLANE, 0, 0, tiled=True)

    message, mods = pl.pallas_call(
        fold_block,
        out_shape=[
            pltpu.VMEM((32, MOD_ROWS, LANES), bf16),
            pltpu.HBM((64, LANES), f32),
        ],
        in_specs=whole(2) + anywhere(1),
        out_specs=whole(2),
        scratch_shapes=[
            pltpu.VMEM((32 * MSG_ROWS, LANES), f32),
            pltpu.VMEM((1536, LANES), f32),
            pltpu.VMEM((1536, LANES), bf16),
            pltpu.VMEM((64, LANES), f32),
            pltpu.VMEM((64, LANES), f32),
        ],
        compiler_params=params,
        name="fold_block",
    )(in_vmem(got), in_vmem(w_in), in_vmem(state))
    wo_half = pl.pallas_call(
        unpack_wo,
        out_shape=pltpu.VMEM((768, 384), bf16),
        in_specs=whole(1) + anywhere(1),
        out_specs=pl.BlockSpec(memory_space=pltpu.VMEM),
        compiler_params=params,
        name="unpack_wo",
    )(in_vmem(got), in_hbm(mods))
    wo_next = lax.ppermute(wo_half, ("s", "w", "c"), neighbour_planes())
    wo_all = [wo_half, wo_next, shifted(wo_half, "c", 1), shifted(wo_next, "c", 1)]
    got = lax.all_to_all(message, PLANE, 0, 0, tiled=True)

    stepped = pl.pallas_call(
        lambda *refs: finish(*refs[:5], refs[5:11], refs[11:15], *refs[15:]),
        out_shape=jax.ShapeDtypeStruct((64, 96), f32),
        in_specs=scalars(2) + whole(3) + anywhere(6) + [pl.BlockSpec(memory_space=pl.ANY)] * 4,
        out_specs=pl.BlockSpec(memory_space=pltpu.VMEM),
        scratch_shapes=[
            pltpu.VMEM((96, 768), bf16),
            pltpu.VMEM((384, 768), bf16),
            pltpu.VMEM((384, 768), bf16),
            pltpu.VMEM((96, 768), bf16),
            pltpu.VMEM((96, 1536), f32),
            pltpu.VMEM((96, 1536), bf16),
            pltpu.VMEM((96, 64), bf16),
            pltpu.VMEM((64, LANES), f32),
            pltpu.VMEM((64, 1536), bf16),
            pltpu.SMEM((STEPS,), jnp.int32),
            pltpu.VMEM((1536, 768), bf16),
            pltpu.SemaphoreType.DMA((22,)),
        ],
        compiler_params=params,
        name="finish",
    )(
        window_start,
        window_count,
        *map(in_vmem, (got, state, w_in)),
        *map(in_hbm, (tokens, cache_keys[0], cache_values[0], mods, w_out.T, timesteps)),
        *wo_all,
    )
    return stepped[None, None]


def solution(mesh):
    grid = Mesh(mesh.devices.reshape(8, 4, 2, 4, 2), ("s", "x", "w", "y", "c"))
    streams = ("x", "w", "y", "c")
    in_specs = (
        P("s", streams, None, None),
        P("s", streams, None, None),
        P(streams, None, "s"),
        P(streams, None, None),
        P(streams, None, None),
        P(streams),
        P(streams),
        P(),
        P(),
        P(None, streams),
        P(("s",) + streams, None),
        P(streams, None),
        P(),
    )
    out_specs = P("s", streams, None, None)
    return jax.shard_map(
        per_device, mesh=grid, in_specs=in_specs, out_specs=out_specs, check_vma=False
    )
```
